32 devices in a mesh: row: 8 (over z, y), col: 4 (over x, core).
Axes of the slice: x: 2, y: 2, z: 4, core: 2. Of those that a mesh axis runs over, the one named last changes fastest.
Arguments:
- integrals: float32 [2048, 20480], P('row', 'col'), may hold values from -6 to 6
- factor: float32 [2048, 2048], P('row', 'col'), may hold values from -1 to 2, as said below
Outputs:
- coefficients: float32 [2048, 20480], P('row', 'col')
The draws below stay inside these ranges and needn't reach their ends.
Inputs may be any that keep to these rules, and one draw needn't show every extreme that they name: factor is zero above its diagonal (column index greater than row index) and between 1 and 2 on it.
All inputs are finite; a program needn't handle non-finite values.
Results may differ from the reference program's by a relative error of at most 0.0001.
Values sent between devices are 32-bit elements; how exact they have to be, the bound alone decides.
A program may use at most 64 MiB of HBM per device.

```python
import jax
import jax.numpy as jnp
from jax import lax

NV = 20480
PANEL = 256
PANELS = 8
ROWS = 2048


def draw_factor(key, part):
    width_all = PANELS * PANEL
    key_noise = jax.random.fold_in(key, 17)
    key_diag = jax.random.fold_in(key, 29)
    row_ids = jnp.arange(ROWS)[:, None]
    col_ids = jnp.arange(width_all)[None, :]
    noise = jax.random.normal(key_noise, (ROWS, width_all), jnp.float32)
    same = row_ids // PANEL == col_ids // PANEL
    spread = jnp.where(same, 0.4 / PANEL ** 0.5, jnp.where(row_ids < width_all, 0.3 / width_all ** 0.5, 1.0 / width_all ** 0.5))
    diagonal = jax.random.uniform(key_diag, (ROWS, 1), jnp.float32, 1.0, 2.0)
    lower = jnp.clip(noise * spread, -0.9, 0.9)
    return jnp.where(row_ids > col_ids, lower, jnp.where(row_ids == col_ids, diagonal, 0.0)).astype(jnp.float32)


def block_scale(own_key, extent, pieces, smallest, largest):
    def one(dim, parts):
        draws = jax.random.uniform(jax.random.fold_in(jax.random.fold_in(own_key, 6), dim), (parts,), jnp.float32, smallest / len(pieces), largest / len(pieces))
        return jnp.repeat(jnp.exp(draws), extent[dim] // parts).reshape((-1,) + (1,) * (len(extent) - dim - 1))

    factor_of = one(*pieces[0])
    for cut in pieces[1:]:
        factor_of = factor_of * one(*cut)
    return factor_of


def normal_values(key, shape, scale, most, pieces=(), held_as=jnp.bfloat16):
    values = scale * jax.random.normal(key, shape, jnp.float32)
    if pieces:
        values = values * block_scale(key, shape, pieces, -0.22, 0.18)
    return jnp.clip(values, -most, most).astype(held_as)


def setup_inputs(seed: int = 0) -> dict:
    streams_of = jax.random.split(jax.random.key(seed), 3)
    integrals = normal_values(streams_of[0], (ROWS, NV), 1.0, 6.0, ((0, 8), (1, 4)), jnp.float32)
    factor = draw_factor(jax.random.fold_in(streams_of[2], 71), 0)
    return {"integrals": integrals, "factor": factor}


def reference(integrals, factor):
    work = integrals
    for panel_index in range(PANELS):
        start = panel_index * PANEL
        stop = start + PANEL
        lower_block = factor[start:stop, start:stop]
        solved = jax.scipy.linalg.solve_triangular(lower_block, work[start:stop], lower=True)
        below = work[stop:] - jnp.dot(factor[stop:, start:stop].astype(jnp.float32), solved.astype(jnp.float32), precision=lax.Precision.HIGHEST, preferred_element_type=jnp.float32)
        work = jnp.concatenate([work[:start], solved, below], axis=0)
    return work
```

```python
import functools

import jax
import jax.numpy as jnp
from jax import lax
from jax.experimental import pallas as pl
from jax.experimental.pallas import tpu as pltpu
from jax.sharding import PartitionSpec as P

MESH = pl.DeviceIdType.MESH
SUB = 128
LANES = 128


def split(value):
    high = value.astype(jnp.bfloat16)
    return high, (value - high.astype(jnp.float32)).astype(jnp.bfloat16)


def dot3(left, right_high, right_low):
    left_high, left_low = split(left)
    mm = functools.partial(jnp.dot, preferred_element_type=jnp.float32)
    return mm(left_high, right_high) + (mm(left_high, right_low) + mm(left_low, right_high))


def invert_lower(block):
    size = block.shape[0]
    mm = functools.partial(
        jnp.dot, precision=lax.Precision.HIGHEST, preferred_element_type=jnp.float32
    )
    rows = lax.broadcasted_iota(jnp.int32, (size, size), 0)
    cols = lax.broadcasted_iota(jnp.int32, (size, size), 1)
    inverse = jnp.where(rows == cols, 1.0 / jnp.where(rows == cols, block, 1.0), 0.0)
    span = 1
    while span < size:
        pair = (rows // (2 * span) == cols // (2 * span)) & (rows // span > cols // span)
        below = jnp.where(pair, block, 0.0)
        inverse = inverse - mm(inverse, mm(below, inverse))
        span *= 2
    return inverse


def invert_kernel(factor_ref, out_ref):
    panel, width = factor_ref.shape
    out_ref[...] = factor_ref[...]
    start = lax.axis_index("row") * panel - lax.axis_index("col") * width
    for offset in range(0, width, panel):

        @pl.when(start == offset)
        def _():
            for sub in range(0, panel, SUB):
                here = slice(sub, sub + SUB)
                there = slice(offset + sub, offset + sub + SUB)
                out_ref[here, there] = invert_lower(factor_ref[here, there])


def greet(peers):
    barrier = pltpu.get_barrier_semaphore()
    me = lax.axis_index("row")
    for step in range(1, peers):
        pl.semaphore_signal(
            barrier, inc=1, device_id={"row": lax.rem(me + step, peers)}, device_id_type=MESH
        )
    pl.semaphore_wait(barrier, peers - 1)


def scatter_kernel(peers, block_ref, out_ref, send_sem, recv_sem, own_sem):
    me = lax.axis_index("row")
    panel = block_ref.shape[0]
    width = out_ref.shape[1]
    greet(peers)

    def piece(peer, owner):
        return pltpu.make_async_remote_copy(
            src_ref=block_ref.at[:, pl.ds(pl.multiple_of(peer * width, LANES), width)],
            dst_ref=out_ref.at[pl.ds(pl.multiple_of(owner * panel, panel), panel), :],
            send_sem=send_sem.at[peer],
            recv_sem=recv_sem.at[owner],
            device_id={"row": peer},
            device_id_type=MESH,
        )

    for step in range(1, peers):
        piece(lax.rem(me + step, peers), me).start()
    own = pltpu.make_async_copy(
        block_ref.at[:, pl.ds(pl.multiple_of(me * width, LANES), width)],
        out_ref.at[pl.ds(pl.multiple_of(me * panel, panel), panel), :],
        own_sem,
    )
    own.start()
    own.wait()
    for step in range(1, peers):
        piece(lax.rem(me + step, peers), me).wait_send()
    for step in range(1, peers):
        owner = lax.rem(me + step, peers)
        piece(owner, owner).wait_recv()


def solve_kernel(
    peers, cols, work_ref, factor_ref, out_ref, solved, high, low, total, send_sem, recv_sem, own_sem
):
    me = lax.axis_index("row")
    panel, span = factor_ref.shape[1:]
    width = work_ref.shape[1]
    panels = cols * span // panel
    here = pl.ds(pl.multiple_of(me * width, LANES), width)
    greet(peers)

    def piece(target, owner):
        return pltpu.make_async_remote_copy(
            src_ref=solved.at[pl.ds(pl.multiple_of(target * panel, panel), panel), :],
            dst_ref=out_ref.at[:, pl.ds(pl.multiple_of(owner * width, LANES), width)],
            send_sem=send_sem.at[target],
            recv_sem=recv_sem.at[owner],
            device_id={"row": target},
            device_id_type=MESH,
        )

    for k in range(peers):
        rows = slice(k * panel, (k + 1) * panel)
        full = min(k * panel // span, cols)
        total[...] = work_ref[rows, :]
        if full:

            @pl.loop(0, full)
            def _(c):
                part = pl.ds(pl.multiple_of(c * span, span), span)
                total[...] -= dot3(factor_ref[k * cols + c], high[part, :], low[part, :])

        if k < panels:
            c, offset = full, k * panel - full * span
            if offset:
                part = slice(c * span, c * span + offset)
                total[...] -= dot3(
                    factor_ref[k * cols + c, :, 0:offset], high[part, :], low[part, :]
                )
            for sub in range(0, panel, SUB):
                value = total[sub : sub + SUB, :]
                if sub:
                    part = slice(k * panel, k * panel + sub)
                    value = value - dot3(
                        factor_ref[k * cols + c, sub : sub + SUB, offset : offset + sub],
                        high[part, :],
                        low[part, :],
                    )
                inverse = factor_ref[
                    k * cols + c, sub : sub + SUB, offset + sub : offset + sub + SUB
                ]
                value = dot3(inverse, *split(value))
                part = slice(k * panel + sub, k * panel + sub + SUB)
                solved[part, :] = value
                high[part, :], low[part, :] = split(value)
        else:
            solved[rows, :] = total[...]

        @pl.when(me != k)
        def _():
            piece(k, me).start()

        @pl.when(me == k)
        def _():
            pltpu.make_async_copy(solved.at[rows, :], out_ref.at[:, here], own_sem).start()

    pltpu.make_async_copy(solved.at[0:panel, :], out_ref.at[:, here], own_sem).wait()
    for step in range(1, peers):
        other = lax.rem(me + step, peers)
        piece(other, me).wait_send()
    for step in range(1, peers):
        other = lax.rem(me + step, peers)
        piece(other, other).wait_recv()


def shards(peers, cols, integrals, factor):
    panel, columns = integrals.shape
    span = factor.shape[1]
    width = -(-columns // (peers * LANES)) * LANES
    rows = peers * panel
    anywhere = pl.BlockSpec(memory_space=pl.ANY)
    vmem = pl.BlockSpec(memory_space=pltpu.VMEM)

    ready = pl.pallas_call(
        invert_kernel,
        out_shape=jax.ShapeDtypeStruct(factor.shape, jnp.float32),
        in_specs=[vmem],
        out_specs=vmem,
    )(factor)
    whole = lax.all_gather(ready, ("row", "col"))

    padded = jnp.pad(integrals, ((0, 0), (0, width * peers - columns)))
    work = pl.pallas_call(
        functools.partial(scatter_kernel, peers),
        out_shape=jax.ShapeDtypeStruct((rows, width), jnp.float32),
        in_specs=[anywhere],
        out_specs=anywhere,
        scratch_shapes=[
            pltpu.SemaphoreType.DMA((peers,)),
            pltpu.SemaphoreType.DMA((peers,)),
            pltpu.SemaphoreType.DMA,
        ],
        compiler_params=pltpu.CompilerParams(collective_id=0, has_side_effects=True),
        cost_estimate=pl.CostEstimate(
            flops=0, bytes_accessed=40 * rows * width * 4, transcendentals=0
        ),
    )(padded)

    out = pl.pallas_call(
        functools.partial(solve_kernel, peers, cols),
        out_shape=jax.ShapeDtypeStruct((panel, width * peers), jnp.float32),
        in_specs=[vmem, vmem],
        out_specs=anywhere,
        scratch_shapes=[
            pltpu.VMEM((rows, width), jnp.float32),
            pltpu.VMEM((cols * span, width), jnp.bfloat16),
            pltpu.VMEM((cols * span, width), jnp.bfloat16),
            pltpu.VMEM((panel, width), jnp.float32),
            pltpu.SemaphoreType.DMA((peers,)),
            pltpu.SemaphoreType.DMA((peers,)),
            pltpu.SemaphoreType.DMA,
        ],
        compiler_params=pltpu.CompilerParams(
            collective_id=1, has_side_effects=True, vmem_limit_bytes=60 * 1024 * 1024
        ),
        cost_estimate=pl.CostEstimate(
            flops=rows * cols * span * width * 3, bytes_accessed=rows * width * 8, transcendentals=0
        ),
    )(work, whole)
    return out[:, :columns]


def solution(mesh):
    placed = (P("row", "col"), P("row", "col"))
    body = functools.partial(shards, mesh.shape["row"], mesh.shape["col"])
    return jax.shard_map(
        body, mesh=mesh, in_specs=placed, out_specs=P("row", "col"), check_vma=False
    )
```

```python
import functools

import jax
import jax.numpy as jnp
from jax import lax
from jax.experimental import pallas as pl
from jax.experimental.pallas import tpu as pltpu
from jax.sharding import PartitionSpec as P

MESH = pl.DeviceIdType.MESH
SUB = 128
LANES = 128


def split(value):
    high = value.astype(jnp.bfloat16)
    return high, (value - high.astype(jnp.float32)).astype(jnp.bfloat16)


def dot3(left, right_high, right_low):
    left_high, left_low = split(left)
    mm = functools.partial(jnp.dot, preferred_element_type=jnp.float32)
    return mm(left_high, right_high) + (mm(left_high, right_low) + mm(left_low, right_high))


def invert_lower(block):
    size = block.shape[0]
    mm = functools.partial(
        jnp.dot, precision=lax.Precision.HIGHEST, preferred_element_type=jnp.float32
    )
    rows = lax.broadcasted_iota(jnp.int32, (size, size), 0)
    cols = lax.broadcasted_iota(jnp.int32, (size, size), 1)
    inverse = jnp.where(rows == cols, 1.0 / jnp.where(rows == cols, block, 1.0), 0.0)
    span = 1
    while span < size:
        pair = (rows // (2 * span) == cols // (2 * span)) & (rows // span > cols // span)
        below = jnp.where(pair, block, 0.0)
        inverse = inverse - mm(inverse, mm(below, inverse))
        span *= 2
    return inverse


def kernel(
    peers,
    cols,
    block_ref,
    factor_ref,
    out_ref,
    work,
    whole,
    solved,
    high,
    low,
    total,
    own_sem,
    there_send,
    there_recv,
    back_send,
    back_recv,
    whole_recv,
    far_send,
    near_send,
    across_send,
    core_send,
):
    me, col = lax.axis_index("row"), lax.axis_index("col")
    panel, span = factor_ref.shape
    width = work.shape[1]
    panels = cols * span // panel
    groups, chips = peers // 2, cols // 2
    group, side = me // 2, lax.rem(me, 2)
    chip, core = col // 2, lax.rem(col, 2)

    def far(step):
        return lax.rem(group + step, groups) * 2

    def across(step):
        return lax.rem(chip + step, chips) * 2 + core

    other_side = {"row": group * 2 + 1 - side}
    other_core = {"col": chip * 2 + 1 - core}

    barrier = pltpu.get_barrier_semaphore()
    friends = [{"row": lax.rem(me + step, peers)} for step in range(1, peers)]
    friends += [{"col": across(step)} for step in range(1, chips)] + [other_core]
    for friend in friends:
        pl.semaphore_signal(barrier, inc=1, device_id=friend, device_id_type=MESH)
    pl.semaphore_wait(barrier, len(friends))

    def rows_of(peer):
        return pl.ds(pl.multiple_of(peer * panel, panel), panel)

    def columns_of(peer):
        return pl.ds(pl.multiple_of(peer * width, LANES), width)

    def send_work(peer, owner):
        return pltpu.make_async_remote_copy(
            src_ref=block_ref.at[:, columns_of(peer)],
            dst_ref=work.at[rows_of(owner), :],
            send_sem=there_send.at[peer],
            recv_sem=there_recv.at[owner],
            device_id={"row": peer},
            device_id_type=MESH,
        )

    def send_solved(target, owner):
        return pltpu.make_async_remote_copy(
            src_ref=solved.at[rows_of(target), :],
            dst_ref=out_ref.at[:, columns_of(owner)],
            send_sem=back_send.at[target],
            recv_sem=back_recv.at[owner],
            device_id={"row": target},
            device_id_type=MESH,
        )

    def send_factor(row, column, sem, device):
        index = row * cols + column
        return pltpu.make_async_remote_copy(
            src_ref=whole.at[index],
            dst_ref=whole.at[index],
            send_sem=sem,
            recv_sem=whole_recv.at[index],
            device_id=device,
            device_id_type=MESH,
        )

    def needed(row, column):
        return column * span < (row + 1) * panel

    def arrived(row, column):
        send_factor(row, column, core_send.at[0], other_core).wait_recv()

    def copies(row, column, own, near, chip_step):
        found = []
        index = row * chips + column // 2
        if own:
            for step in range(1, groups):
                found.append(
                    send_factor(row, column, far_send.at[step], {"row": far(step) + side})
                )
        if near:
            found.append(send_factor(row, column, near_send.at[row // 2], other_side))
        if chip_step == 0:
            for step in range(1, chips):
                sem = across_send.at[row * chips + step]
                found.append(send_factor(row, column, sem, {"col": across(step)}))
        found.append(send_factor(row, column, core_send.at[index], other_core))
        return found

    relayed = [(me, col, True, True, 0)]
    relayed += [(far(step) + side, col, False, True, 0) for step in range(1, groups)]
    relayed += [(far(step) + 1 - side, col, False, False, 0) for step in range(groups)]
    for step in range(1, chips):
        relayed += [(row, across(step), False, False, step) for row in range(peers)]

    for step in range(1, peers):
        send_work(lax.rem(me + step, peers), me).start()
    own = pltpu.make_async_copy(
        block_ref.at[:, columns_of(me)], work.at[rows_of(me), :], own_sem
    )
    own.start()

    mine = me * cols + col
    whole[mine] = factor_ref[...]
    start = me * panel - col * span
    for offset in range(0, span, panel):

        @pl.when(start == offset)
        def _():
            for sub in range(0, panel, SUB):
                there = slice(offset + sub, offset + sub + SUB)
                whole[mine, sub : sub + SUB, there] = invert_lower(
                    factor_ref[sub : sub + SUB, there]
                )

    for row, column, is_own, near, chip_step in relayed:

        @pl.when(needed(row, column))
        def _():
            if not is_own:
                arrived(row, column)
            for copy in copies(row, column, is_own, near, chip_step):
                copy.start()

    own.wait()

    for k in range(peers):
        rows = slice(k * panel, (k + 1) * panel)
        full = min(k * panel // span, cols)

        @pl.when(me != k)
        def _():
            send_work(k, k).wait_recv()

        for step in range(chips):
            column = step * 2 + 1 - core

            @pl.when(needed(k, column))
            def _():
                arrived(k, column)

        total[...] = work[rows, :]
        if full:

            @pl.loop(0, full)
            def _(c):
                part = pl.ds(pl.multiple_of(c * span, span), span)
                total[...] -= dot3(whole[k * cols + c], high[part, :], low[part, :])

        if k < panels:
            c, offset = full, k * panel - full * span
            if offset:
                part = slice(c * span, c * span + offset)
                total[...] -= dot3(whole[k * cols + c, :, 0:offset], high[part, :], low[part, :])
            for sub in range(0, panel, SUB):
                value = total[sub : sub + SUB, :]
                if sub:
                    part = slice(k * panel, k * panel + sub)
                    value = value - dot3(
                        whole[k * cols + c, sub : sub + SUB, offset : offset + sub],
                        high[part, :],
                        low[part, :],
                    )
                inverse = whole[k * cols + c, sub : sub + SUB, offset + sub : offset + sub + SUB]
                value = dot3(inverse, *split(value))
                part = slice(k * panel + sub, k * panel + sub + SUB)
                solved[part, :] = value
                high[part, :], low[part, :] = split(value)
        else:
            solved[rows, :] = total[...]

        @pl.when(me != k)
        def _():
            send_solved(k, me).start()

        @pl.when(me == k)
        def _():
            pltpu.make_async_copy(solved.at[rows, :], out_ref.at[:, columns_of(me)], own_sem).start()

    pltpu.make_async_copy(solved.at[0:panel, :], out_ref.at[:, columns_of(me)], own_sem).wait()
    for row, column, is_own, near, chip_step in relayed:

        @pl.when(needed(row, column))
        def _():
            for copy in copies(row, column, is_own, near, chip_step):
                copy.wait_send()

    for step in range(1, peers):
        other = lax.rem(me + step, peers)
        send_work(other, me).wait_send()
        send_solved(other, me).wait_send()
    for step in range(1, peers):
        other = lax.rem(me + step, peers)
        send_solved(other, other).wait_recv()


def shards(peers, cols, integrals, factor):
    panel, columns = integrals.shape
    span = factor.shape[1]
    width = -(-columns // (peers * LANES)) * LANES
    rows = peers * panel
    anywhere = pl.BlockSpec(memory_space=pl.ANY)
    padded = jnp.pad(integrals, ((0, 0), (0, width * peers - columns)))
    dma = pltpu.SemaphoreType.DMA
    out = pl.pallas_call(
        functools.partial(kernel, peers, cols),
        out_shape=jax.ShapeDtypeStruct((panel, width * peers), jnp.float32),
        in_specs=[anywhere, pl.BlockSpec(memory_space=pltpu.VMEM)],
        out_specs=anywhere,
        scratch_shapes=[
            pltpu.VMEM((rows, width), jnp.float32),
            pltpu.VMEM((peers * cols, panel, span), jnp.float32),
            pltpu.VMEM((rows, width), jnp.float32),
            pltpu.VMEM((cols * span, width), jnp.bfloat16),
            pltpu.VMEM((cols * span, width), jnp.bfloat16),
            pltpu.VMEM((panel, width), jnp.float32),
            dma,
            dma((peers,)),
            dma((peers,)),
            dma((peers,)),
            dma((peers,)),
            dma((peers * cols,)),
            dma((peers // 2,)),
            dma((peers // 2,)),
            dma((peers * cols // 2,)),
            dma((peers * cols // 2,)),
        ],
        compiler_params=pltpu.CompilerParams(
            collective_id=0, has_side_effects=True, vmem_limit_bytes=60 * 1024 * 1024
        ),
        cost_estimate=pl.CostEstimate(
            flops=rows * cols * span * width * 3, bytes_accessed=rows * width * 8, transcendentals=0
        ),
    )(padded, factor)
    return out[:, :columns]


def solution(mesh):
    placed = (P("row", "col"), P("row", "col"))
    body = functools.partial(shards, mesh.shape["row"], mesh.shape["col"])
    return jax.shard_map(
        body, mesh=mesh, in_specs=placed, out_specs=P("row", "col"), check_vma=False
    )
```

```python
import functools

import jax
import jax.numpy as jnp
from jax import lax
from jax.experimental import pallas as pl
from jax.experimental.pallas import tpu as pltpu
from jax.sharding import PartitionSpec as P

MESH = pl.DeviceIdType.MESH
SUB = 128
LANES = 128
AHEAD = 2


def split(value):
    high = value.astype(jnp.bfloat16)
    return high, (value - high.astype(jnp.float32)).astype(jnp.bfloat16)


def dot3(left, right_high, right_low):
    left_high, left_low = split(left)
    mm = functools.partial(jnp.dot, preferred_element_type=jnp.float32)
    return mm(left_high, right_high) + (mm(left_high, right_low) + mm(left_low, right_high))


def invert_lower(block):
    size = block.shape[0]
    mm = functools.partial(
        jnp.dot, precision=lax.Precision.HIGHEST, preferred_element_type=jnp.float32
    )
    rows = lax.broadcasted_iota(jnp.int32, (size, size), 0)
    cols = lax.broadcasted_iota(jnp.int32, (size, size), 1)
    inverse = jnp.where(rows == cols, 1.0 / jnp.where(rows == cols, block, 1.0), 0.0)
    span = 1
    while span < size:
        pair = (rows // (2 * span) == cols // (2 * span)) & (rows // span > cols // span)
        below = jnp.where(pair, block, 0.0)
        inverse = inverse - mm(inverse, mm(below, inverse))
        span *= 2
    return inverse


def kernel(
    peers,
    cols,
    block_ref,
    factor_ref,
    out_ref,
    work,
    whole,
    solved,
    high,
    low,
    total,
    own_sem,
    there_send,
    there_recv,
    back_send,
    back_recv,
    whole_recv,
    far_send,
    near_send,
    across_send,
    core_send,
):
    me, col = lax.axis_index("row"), lax.axis_index("col")
    panel, span = factor_ref.shape
    width = work.shape[1]
    panels = cols * span // panel
    groups, chips = peers // 2, cols // 2
    group, side = me // 2, lax.rem(me, 2)
    chip, core = col // 2, lax.rem(col, 2)

    def far(step):
        return lax.rem(group + step, groups) * 2

    def across(step):
        return lax.rem(chip + step, chips) * 2 + core

    other_side = {"row": group * 2 + 1 - side}
    other_core = {"col": chip * 2 + 1 - core}

    barrier = pltpu.get_barrier_semaphore()
    friends = [{"row": lax.rem(me + step, peers)} for step in range(1, peers)]
    friends += [{"col": across(step)} for step in range(1, chips)] + [other_core]
    for friend in friends:
        pl.semaphore_signal(barrier, inc=1, device_id=friend, device_id_type=MESH)
    pl.semaphore_wait(barrier, len(friends))

    def rows_of(peer):
        return pl.ds(pl.multiple_of(peer * panel, panel), panel)

    def columns_of(peer):
        return pl.ds(pl.multiple_of(peer * width, LANES), width)

    def send_work(peer, owner):
        return pltpu.make_async_remote_copy(
            src_ref=block_ref.at[:, columns_of(peer)],
            dst_ref=work.at[rows_of(owner), :],
            send_sem=there_send.at[peer],
            recv_sem=there_recv.at[owner],
            device_id={"row": peer},
            device_id_type=MESH,
        )

    def send_solved(target, owner):
        return pltpu.make_async_remote_copy(
            src_ref=solved.at[rows_of(target), :],
            dst_ref=out_ref.at[:, columns_of(owner)],
            send_sem=back_send.at[target],
            recv_sem=back_recv.at[owner],
            device_id={"row": target},
            device_id_type=MESH,
        )

    def send_factor(row, column, sem, device):
        index = row * cols + column
        return pltpu.make_async_remote_copy(
            src_ref=whole.at[index],
            dst_ref=whole.at[index],
            send_sem=sem,
            recv_sem=whole_recv.at[index],
            device_id=device,
            device_id_type=MESH,
        )

    def needed(row, column):
        return column * span < (row + 1) * panel

    def arrived(row, column):
        send_factor(row, column, core_send.at[0], other_core).wait_recv()

    def copies(row, column, own, near, chip_step):
        found = []
        index = row * chips + column // 2
        if own:
            for step in range(1, groups):
                found.append(
                    send_factor(row, column, far_send.at[step], {"row": far(step) + side})
                )
        if near:
            found.append(send_factor(row, column, near_send.at[row // 2], other_side))
        if chip_step == 0:
            for step in range(1, chips):
                sem = across_send.at[row * chips + step]
                found.append(send_factor(row, column, sem, {"col": across(step)}))
        found.append(send_factor(row, column, core_send.at[index], other_core))
        return found

    relayed = [(me, col, True, True, 0)]
    relayed += [(far(step) + side, col, False, True, 0) for step in range(1, groups)]
    relayed += [(far(step) + 1 - side, col, False, False, 0) for step in range(groups)]
    for step in range(1, chips):
        relayed += [(row, across(step), False, False, step) for row in range(peers)]

    own = pltpu.make_async_copy(
        block_ref.at[:, columns_of(me)], work.at[rows_of(me), :], own_sem
    )
    own.start()

    mine = me * cols + col
    whole[mine] = factor_ref[...]
    start = me * panel - col * span
    for offset in range(0, span, panel):

        @pl.when(start == offset)
        def _():
            for sub in range(0, panel, SUB):
                there = slice(offset + sub, offset + sub + SUB)
                whole[mine, sub : sub + SUB, there] = invert_lower(
                    factor_ref[sub : sub + SUB, there]
                )

    waiting = list(range(1, peers))
    for row, column, is_own, near, chip_step in relayed:

        @pl.when(needed(row, column))
        def _():
            if not is_own:
                arrived(row, column)
            for copy in copies(row, column, is_own, near, chip_step):
                copy.start()

        for _ in range(AHEAD if is_own else 1):
            if waiting:
                send_work(lax.rem(me + waiting.pop(0), peers), me).start()

    for step in waiting:
        send_work(lax.rem(me + step, peers), me).start()
    own.wait()

    for k in range(peers):
        rows = slice(k * panel, (k + 1) * panel)
        full = min(k * panel // span, cols)

        @pl.when(me != k)
        def _():
            send_work(k, k).wait_recv()

        for step in range(chips):
            column = step * 2 + 1 - core

            @pl.when(needed(k, column))
            def _():
                arrived(k, column)

        total[...] = work[rows, :]
        if full:

            @pl.loop(0, full)
            def _(c):
                part = pl.ds(pl.multiple_of(c * span, span), span)
                total[...] -= dot3(whole[k * cols + c], high[part, :], low[part, :])

        if k < panels:
            c, offset = full, k * panel - full * span
            if offset:
                part = slice(c * span, c * span + offset)
                total[...] -= dot3(whole[k * cols + c, :, 0:offset], high[part, :], low[part, :])
            for sub in range(0, panel, SUB):
                value = total[sub : sub + SUB, :]
                if sub:
                    part = slice(k * panel, k * panel + sub)
                    value = value - dot3(
                        whole[k * cols + c, sub : sub + SUB, offset : offset + sub],
                        high[part, :],
                        low[part, :],
                    )
                inverse = whole[k * cols + c, sub : sub + SUB, offset + sub : offset + sub + SUB]
                value = dot3(inverse, *split(value))
                part = slice(k * panel + sub, k * panel + sub + SUB)
                solved[part, :] = value
                high[part, :], low[part, :] = split(value)
        else:
            solved[rows, :] = total[...]

        @pl.when(me != k)
        def _():
            send_solved(k, me).start()

        @pl.when(me == k)
        def _():
            pltpu.make_async_copy(solved.at[rows, :], out_ref.at[:, columns_of(me)], own_sem).start()

    pltpu.make_async_copy(solved.at[0:panel, :], out_ref.at[:, columns_of(me)], own_sem).wait()
    for row, column, is_own, near, chip_step in relayed:

        @pl.when(needed(row, column))
        def _():
            for copy in copies(row, column, is_own, near, chip_step):
                copy.wait_send()

    for step in range(1, peers):
        other = lax.rem(me + step, peers)
        send_work(other, me).wait_send()
        send_solved(other, me).wait_send()
    for step in range(1, peers):
        other = lax.rem(me + step, peers)
        send_solved(other, other).wait_recv()


def shards(peers, cols, integrals, factor):
    panel, columns = integrals.shape
    span = factor.shape[1]
    width = -(-columns // (peers * LANES)) * LANES
    rows = peers * panel
    anywhere = pl.BlockSpec(memory_space=pl.ANY)
    padded = jnp.pad(integrals, ((0, 0), (0, width * peers - columns)))
    dma = pltpu.SemaphoreType.DMA
    out = pl.pallas_call(
        functools.partial(kernel, peers, cols),
        out_shape=jax.ShapeDtypeStruct((panel, width * peers), jnp.float32),
        in_specs=[anywhere, pl.BlockSpec(memory_space=pltpu.VMEM)],
        out_specs=anywhere,
        scratch_shapes=[
            pltpu.VMEM((rows, width), jnp.float32),
            pltpu.VMEM((peers * cols, panel, span), jnp.float32),
            pltpu.VMEM((rows, width), jnp.float32),
            pltpu.VMEM((cols * span, width), jnp.bfloat16),
            pltpu.VMEM((cols * span, width), jnp.bfloat16),
            pltpu.VMEM((panel, width), jnp.float32),
            dma,
            dma((peers,)),
            dma((peers,)),
            dma((peers,)),
            dma((peers,)),
            dma((peers * cols,)),
            dma((peers // 2,)),
            dma((peers // 2,)),
            dma((peers * cols // 2,)),
            dma((peers * cols // 2,)),
        ],
        compiler_params=pltpu.CompilerParams(
            collective_id=0, has_side_effects=True, vmem_limit_bytes=60 * 1024 * 1024
        ),
        cost_estimate=pl.CostEstimate(
            flops=rows * cols * span * width * 3, bytes_accessed=rows * width * 8, transcendentals=0
        ),
    )(padded, factor)
    return out[:, :columns]


def solution(mesh):
    placed = (P("row", "col"), P("row", "col"))
    body = functools.partial(shards, mesh.shape["row"], mesh.shape["col"])
    return jax.shard_map(
        body, mesh=mesh, in_specs=placed, out_specs=P("row", "col"), check_vma=False
    )
```

```python
import functools

import jax
import jax.numpy as jnp
from jax import lax
from jax.experimental import pallas as pl
from jax.experimental.pallas import tpu as pltpu
from jax.sharding import PartitionSpec as P

MESH = pl.DeviceIdType.MESH
SUB = 128
LANES = 128
AHEAD = 4


def split(value):
    high = value.astype(jnp.bfloat16)
    return high, (value - high.astype(jnp.float32)).astype(jnp.bfloat16)


def dot3(left, right_high, right_low):
    left_high, left_low = split(left)
    mm = functools.partial(jnp.dot, preferred_element_type=jnp.float32)
    return mm(left_high, right_high) + (mm(left_high, right_low) + mm(left_low, right_high))


def invert_lower(block):
    size = block.shape[0]
    mm = functools.partial(
        jnp.dot, precision=lax.Precision.HIGHEST, preferred_element_type=jnp.float32
    )
    rows = lax.broadcasted_iota(jnp.int32, (size, size), 0)
    cols = lax.broadcasted_iota(jnp.int32, (size, size), 1)
    inverse = jnp.where(rows == cols, 1.0 / jnp.where(rows == cols, block, 1.0), 0.0)
    span = 1
    while span < size:
        pair = (rows // (2 * span) == cols // (2 * span)) & (rows // span > cols // span)
        below = jnp.where(pair, block, 0.0)
        inverse = inverse - mm(inverse, mm(below, inverse))
        span *= 2
    return inverse


def kernel(
    peers,
    cols,
    block_ref,
    factor_ref,
    out_ref,
    work,
    whole,
    solved,
    high,
    low,
    total,
    own_sem,
    there_send,
    there_recv,
    back_send,
    back_recv,
    whole_recv,
    far_send,
    near_send,
    across_send,
    core_send,
):
    me, col = lax.axis_index("row"), lax.axis_index("col")
    panel, span = factor_ref.shape
    width = work.shape[1]
    panels = cols * span // panel
    groups, chips = peers // 2, cols // 2
    group, side = me // 2, lax.rem(me, 2)
    chip, core = col // 2, lax.rem(col, 2)

    def far(step):
        return lax.rem(group + step, groups) * 2

    def across(step):
        return lax.rem(chip + step, chips) * 2 + core

    other_side = {"row": group * 2 + 1 - side}
    other_core = {"col": chip * 2 + 1 - core}

    barrier = pltpu.get_barrier_semaphore()
    friends = [{"row": lax.rem(me + step, peers)} for step in range(1, peers)]
    friends += [{"col": across(step)} for step in range(1, chips)] + [other_core]
    for friend in friends:
        pl.semaphore_signal(barrier, inc=1, device_id=friend, device_id_type=MESH)
    pl.semaphore_wait(barrier, len(friends))

    def rows_of(peer):
        return pl.ds(pl.multiple_of(peer * panel, panel), panel)

    def columns_of(peer):
        return pl.ds(pl.multiple_of(peer * width, LANES), width)

    def send_work(peer, owner):
        return pltpu.make_async_remote_copy(
            src_ref=block_ref.at[:, columns_of(peer)],
            dst_ref=work.at[rows_of(owner), :],
            send_sem=there_send.at[peer],
            recv_sem=there_recv.at[owner],
            device_id={"row": peer},
            device_id_type=MESH,
        )

    def send_solved(target, owner):
        return pltpu.make_async_remote_copy(
            src_ref=solved.at[rows_of(target), :],
            dst_ref=out_ref.at[:, columns_of(owner)],
            send_sem=back_send.at[target],
            recv_sem=back_recv.at[owner],
            device_id={"row": target},
            device_id_type=MESH,
        )

    def send_factor(row, column, sem, device):
        index = row * cols + column
        return pltpu.make_async_remote_copy(
            src_ref=whole.at[index],
            dst_ref=whole.at[index],
            send_sem=sem,
            recv_sem=whole_recv.at[index],
            device_id=device,
            device_id_type=MESH,
        )

    def needed(row, column):
        return column * span < (row + 1) * panel

    def arrived(row, column):
        send_factor(row, column, core_send.at[0], other_core).wait_recv()

    def copies(row, column, own, near, chip_step):
        found = []
        index = row * chips + column // 2
        if own:
            for step in range(1, groups):
                found.append(
                    send_factor(row, column, far_send.at[step], {"row": far(step) + side})
                )
        if near:
            found.append(send_factor(row, column, near_send.at[row // 2], other_side))
        if chip_step == 0:
            for step in range(1, chips):
                sem = across_send.at[row * chips + step]
                found.append(send_factor(row, column, sem, {"col": across(step)}))
        found.append(send_factor(row, column, core_send.at[index], other_core))
        return found

    relayed = [(me, col, True, True, 0)]
    relayed += [(far(step) + side, col, False, True, 0) for step in range(1, groups)]
    relayed += [(far(step) + 1 - side, col, False, False, 0) for step in range(groups)]
    for step in range(1, chips):
        relayed += [(row, across(step), False, False, step) for row in range(peers)]

    own = pltpu.make_async_copy(
        block_ref.at[:, columns_of(me)], work.at[rows_of(me), :], own_sem
    )
    own.start()

    mine = me * cols + col
    whole[mine] = factor_ref[...]
    start = me * panel - col * span
    for offset in range(0, span, panel):

        @pl.when(start == offset)
        def _():
            for sub in range(0, panel, SUB):
                there = slice(offset + sub, offset + sub + SUB)
                whole[mine, sub : sub + SUB, there] = invert_lower(
                    factor_ref[sub : sub + SUB, there]
                )

    waiting = list(range(1, peers))
    for row, column, is_own, near, chip_step in relayed:

        @pl.when(needed(row, column))
        def _():
            if not is_own:
                arrived(row, column)
            for copy in copies(row, column, is_own, near, chip_step):
                copy.start()

        for _ in range(AHEAD if is_own else 1):
            if waiting:
                send_work(lax.rem(me + waiting.pop(0), peers), me).start()

    for step in waiting:
        send_work(lax.rem(me + step, peers), me).start()
    own.wait()

    for k in range(peers):
        rows = slice(k * panel, (k + 1) * panel)
        full = min(k * panel // span, cols)

        @pl.when(me != k)
        def _():
            send_work(k, k).wait_recv()

        for step in range(chips):
            column = step * 2 + 1 - core

            @pl.when(needed(k, column))
            def _():
                arrived(k, column)

        total[...] = work[rows, :]
        if full:

            @pl.loop(0, full)
            def _(c):
                part = pl.ds(pl.multiple_of(c * span, span), span)
                total[...] -= dot3(whole[k * cols + c], high[part, :], low[part, :])

        if k < panels:
            c, offset = full, k * panel - full * span
            if offset:
                part = slice(c * span, c * span + offset)
                total[...] -= dot3(whole[k * cols + c, :, 0:offset], high[part, :], low[part, :])
            for sub in range(0, panel, SUB):
                value = total[sub : sub + SUB, :]
                if sub:
                    part = slice(k * panel, k * panel + sub)
                    value = value - dot3(
                        whole[k * cols + c, sub : sub + SUB, offset : offset + sub],
                        high[part, :],
                        low[part, :],
                    )
                inverse = whole[k * cols + c, sub : sub + SUB, offset + sub : offset + sub + SUB]
                value = dot3(inverse, *split(value))
                part = slice(k * panel + sub, k * panel + sub + SUB)
                solved[part, :] = value
                high[part, :], low[part, :] = split(value)
        else:
            solved[rows, :] = total[...]

        @pl.when(me != k)
        def _():
            send_solved(k, me).start()

        @pl.when(me == k)
        def _():
            pltpu.make_async_copy(solved.at[rows, :], out_ref.at[:, columns_of(me)], own_sem).start()

    pltpu.make_async_copy(solved.at[0:panel, :], out_ref.at[:, columns_of(me)], own_sem).wait()
    for row, column, is_own, near, chip_step in relayed:

        @pl.when(needed(row, column))
        def _():
            for copy in copies(row, column, is_own, near, chip_step):
                copy.wait_send()

    for step in range(1, peers):
        other = lax.rem(me + step, peers)
        send_work(other, me).wait_send()
        send_solved(other, me).wait_send()
    for step in range(1, peers):
        other = lax.rem(me + step, peers)
        send_solved(other, other).wait_recv()


def shards(peers, cols, integrals, factor):
    panel, columns = integrals.shape
    span = factor.shape[1]
    width = -(-columns // (peers * LANES)) * LANES
    rows = peers * panel
    anywhere = pl.BlockSpec(memory_space=pl.ANY)
    padded = jnp.pad(integrals, ((0, 0), (0, width * peers - columns)))
    dma = pltpu.SemaphoreType.DMA
    out = pl.pallas_call(
        functools.partial(kernel, peers, cols),
        out_shape=jax.ShapeDtypeStruct((panel, width * peers), jnp.float32),
        in_specs=[anywhere, pl.BlockSpec(memory_space=pltpu.VMEM)],
        out_specs=anywhere,
        scratch_shapes=[
            pltpu.VMEM((rows, width), jnp.float32),
            pltpu.VMEM((peers * cols, panel, span), jnp.float32),
            pltpu.VMEM((rows, width), jnp.float32),
            pltpu.VMEM((cols * span, width), jnp.bfloat16),
            pltpu.VMEM((cols * span, width), jnp.bfloat16),
            pltpu.VMEM((panel, width), jnp.float32),
            dma,
            dma((peers,)),
            dma((peers,)),
            dma((peers,)),
            dma((peers,)),
            dma((peers * cols,)),
            dma((peers // 2,)),
            dma((peers // 2,)),
            dma((peers * cols // 2,)),
            dma((peers * cols // 2,)),
        ],
        compiler_params=pltpu.CompilerParams(
            collective_id=0, has_side_effects=True, vmem_limit_bytes=60 * 1024 * 1024
        ),
        cost_estimate=pl.CostEstimate(
            flops=rows * cols * span * width * 3, bytes_accessed=rows * width * 8, transcendentals=0
        ),
    )(padded, factor)
    return out[:, :columns]


def solution(mesh):
    placed = (P("row", "col"), P("row", "col"))
    body = functools.partial(shards, mesh.shape["row"], mesh.shape["col"])
    return jax.shard_map(
        body, mesh=mesh, in_specs=placed, out_specs=P("row", "col"), check_vma=False
    )
```

```python
import functools

import jax
import jax.numpy as jnp
from jax import lax
from jax.experimental import pallas as pl
from jax.experimental.pallas import tpu as pltpu
from jax.sharding import PartitionSpec as P

MESH = pl.DeviceIdType.MESH
SUB = 128
LANES = 128
AHEAD = 2


def split(value):
    high = value.astype(jnp.bfloat16)
    return high, (value - high.astype(jnp.float32)).astype(jnp.bfloat16)


def dot3(left, right_high, right_low):
    left_high, left_low = split(left)
    mm = functools.partial(jnp.dot, preferred_element_type=jnp.float32)
    return mm(left_high, right_high) + (mm(left_high, right_low) + mm(left_low, right_high))


def invert_lower(block):
    size = block.shape[0]
    mm = functools.partial(
        jnp.dot, precision=lax.Precision.HIGHEST, preferred_element_type=jnp.float32
    )
    rows = lax.broadcasted_iota(jnp.int32, (size, size), 0)
    cols = lax.broadcasted_iota(jnp.int32, (size, size), 1)
    inverse = jnp.where(rows == cols, 1.0 / jnp.where(rows == cols, block, 1.0), 0.0)
    span = 1
    while span < size:
        pair = (rows // (2 * span) == cols // (2 * span)) & (rows // span > cols // span)
        below = jnp.where(pair, block, 0.0)
        inverse = inverse - mm(inverse, mm(below, inverse))
        span *= 2
    return inverse


def kernel(
    peers,
    cols,
    block_ref,
    factor_ref,
    out_ref,
    work,
    whole,
    solved,
    high,
    low,
    total,
    own_sem,
    there_send,
    there_recv,
    back_send,
    back_recv,
    whole_recv,
    far_send,
    near_send,
    across_send,
    core_send,
):
    me, col = lax.axis_index("row"), lax.axis_index("col")
    panel, span = factor_ref.shape
    width = work.shape[1]
    panels = cols * span // panel
    groups, chips = peers // 2, cols // 2
    group, side = me // 2, lax.rem(me, 2)
    chip, core = col // 2, lax.rem(col, 2)

    def far(step):
        return lax.rem(group + step, groups) * 2

    def across(step):
        return lax.rem(chip + step, chips) * 2 + core

    other_side = {"row": group * 2 + 1 - side}
    other_core = {"col": chip * 2 + 1 - core}

    barrier = pltpu.get_barrier_semaphore()
    friends = [{"row": lax.rem(me + step, peers)} for step in range(1, peers)]
    friends += [{"col": across(step)} for step in range(1, chips)] + [other_core]
    for friend in friends:
        pl.semaphore_signal(barrier, inc=1, device_id=friend, device_id_type=MESH)
    pl.semaphore_wait(barrier, len(friends))

    def rows_of(peer):
        return pl.ds(pl.multiple_of(peer * panel, panel), panel)

    def columns_of(peer):
        return pl.ds(pl.multiple_of(peer * width, LANES), width)

    def send_work(peer, owner):
        return pltpu.make_async_remote_copy(
            src_ref=block_ref.at[:, columns_of(peer)],
            dst_ref=work.at[rows_of(owner), :],
            send_sem=there_send.at[peer],
            recv_sem=there_recv.at[owner],
            device_id={"row": peer},
            device_id_type=MESH,
        )

    def send_solved(target, owner):
        return pltpu.make_async_remote_copy(
            src_ref=solved.at[rows_of(target), :],
            dst_ref=out_ref.at[:, columns_of(owner)],
            send_sem=back_send.at[target],
            recv_sem=back_recv.at[owner],
            device_id={"row": target},
            device_id_type=MESH,
        )

    def send_factor(row, column, sem, device):
        index = row * cols + column
        return pltpu.make_async_remote_copy(
            src_ref=whole.at[index],
            dst_ref=whole.at[index],
            send_sem=sem,
            recv_sem=whole_recv.at[index],
            device_id=device,
            device_id_type=MESH,
        )

    def needed(row, column):
        return column * span < (row + 1) * panel

    def arrived(row, column):
        send_factor(row, column, core_send.at[0], other_core).wait_recv()

    def copies(row, column, own, near, chip_step):
        found = []
        index = row * chips + column // 2
        if own:
            for step in range(1, groups):
                found.append(
                    send_factor(row, column, far_send.at[step], {"row": far(step) + side})
                )
        if near:
            found.append(send_factor(row, column, near_send.at[row // 2], other_side))
        if chip_step == 0:
            for step in range(1, chips):
                sem = across_send.at[row * chips + step]
                found.append(send_factor(row, column, sem, {"col": across(step)}))
        found.append(send_factor(row, column, core_send.at[index], other_core))
        return found

    relayed = [(me, col, True, True, 0)]
    relayed += [(far(step) + side, col, False, True, 0) for step in range(1, groups)]
    relayed += [(far(step) + 1 - side, col, False, False, 0) for step in range(groups)]
    for step in range(1, chips):
        relayed += [(row, across(step), False, False, step) for row in range(peers)]

    own = pltpu.make_async_copy(
        block_ref.at[:, columns_of(me)], work.at[rows_of(me), :], own_sem
    )
    own.start()

    mine = me * cols + col
    whole[mine] = factor_ref[...]
    start = me * panel - col * span
    for offset in range(0, span, panel):

        @pl.when(start == offset)
        def _():
            for sub in range(0, panel, SUB):
                there = slice(offset + sub, offset + sub + SUB)
                whole[mine, sub : sub + SUB, there] = invert_lower(
                    factor_ref[sub : sub + SUB, there]
                )

    waiting = sorted(range(1, peers), key=lambda step: abs(2 * step - peers))
    for row, column, is_own, near, chip_step in relayed:

        @pl.when(needed(row, column))
        def _():
            if not is_own:
                arrived(row, column)
            for copy in copies(row, column, is_own, near, chip_step):
                copy.start()

        for _ in range(AHEAD if is_own else 1):
            if waiting:
                send_work(lax.rem(me + waiting.pop(0), peers), me).start()

    for step in waiting:
        send_work(lax.rem(me + step, peers), me).start()
    own.wait()

    for k in range(peers):
        rows = slice(k * panel, (k + 1) * panel)
        full = min(k * panel // span, cols)

        @pl.when(me != k)
        def _():
            send_work(k, k).wait_recv()

        for step in range(chips):
            column = step * 2 + 1 - core

            @pl.when(needed(k, column))
            def _():
                arrived(k, column)

        total[...] = work[rows, :]
        if full:

            @pl.loop(0, full)
            def _(c):
                part = pl.ds(pl.multiple_of(c * span, span), span)
                total[...] -= dot3(whole[k * cols + c], high[part, :], low[part, :])

        if k < panels:
            c, offset = full, k * panel - full * span
            if offset:
                part = slice(c * span, c * span + offset)
                total[...] -= dot3(whole[k * cols + c, :, 0:offset], high[part, :], low[part, :])
            for sub in range(0, panel, SUB):
                value = total[sub : sub + SUB, :]
                if sub:
                    part = slice(k * panel, k * panel + sub)
                    value = value - dot3(
                        whole[k * cols + c, sub : sub + SUB, offset : offset + sub],
                        high[part, :],
                        low[part, :],
                    )
                inverse = whole[k * cols + c, sub : sub + SUB, offset + sub : offset + sub + SUB]
                value = dot3(inverse, *split(value))
                part = slice(k * panel + sub, k * panel + sub + SUB)
                solved[part, :] = value
                high[part, :], low[part, :] = split(value)
        else:
            solved[rows, :] = total[...]

        @pl.when(me != k)
        def _():
            send_solved(k, me).start()

        @pl.when(me == k)
        def _():
            pltpu.make_async_copy(solved.at[rows, :], out_ref.at[:, columns_of(me)], own_sem).start()

    pltpu.make_async_copy(solved.at[0:panel, :], out_ref.at[:, columns_of(me)], own_sem).wait()
    for row, column, is_own, near, chip_step in relayed:

        @pl.when(needed(row, column))
        def _():
            for copy in copies(row, column, is_own, near, chip_step):
                copy.wait_send()

    for step in range(1, peers):
        other = lax.rem(me + step, peers)
        send_work(other, me).wait_send()
        send_solved(other, me).wait_send()
    for step in range(1, peers):
        other = lax.rem(me + step, peers)
        send_solved(other, other).wait_recv()


def shards(peers, cols, integrals, factor):
    panel, columns = integrals.shape
    span = factor.shape[1]
    width = -(-columns // (peers * LANES)) * LANES
    rows = peers * panel
    anywhere = pl.BlockSpec(memory_space=pl.ANY)
    padded = jnp.pad(integrals, ((0, 0), (0, width * peers - columns)))
    dma = pltpu.SemaphoreType.DMA
    out = pl.pallas_call(
        functools.partial(kernel, peers, cols),
        out_shape=jax.ShapeDtypeStruct((panel, width * peers), jnp.float32),
        in_specs=[anywhere, pl.BlockSpec(memory_space=pltpu.VMEM)],
        out_specs=anywhere,
        scratch_shapes=[
            pltpu.VMEM((rows, width), jnp.float32),
            pltpu.VMEM((peers * cols, panel, span), jnp.float32),
            pltpu.VMEM((rows, width), jnp.float32),
            pltpu.VMEM((cols * span, width), jnp.bfloat16),
            pltpu.VMEM((cols * span, width), jnp.bfloat16),
            pltpu.VMEM((panel, width), jnp.float32),
            dma,
            dma((peers,)),
            dma((peers,)),
            dma((peers,)),
            dma((peers,)),
            dma((peers * cols,)),
            dma((peers // 2,)),
            dma((peers // 2,)),
            dma((peers * cols // 2,)),
            dma((peers * cols // 2,)),
        ],
        compiler_params=pltpu.CompilerParams(
            collective_id=0, has_side_effects=True, vmem_limit_bytes=60 * 1024 * 1024
        ),
        cost_estimate=pl.CostEstimate(
            flops=rows * cols * span * width * 3, bytes_accessed=rows * width * 8, transcendentals=0
        ),
    )(padded, factor)
    return out[:, :columns]


def solution(mesh):
    placed = (P("row", "col"), P("row", "col"))
    body = functools.partial(shards, mesh.shape["row"], mesh.shape["col"])
    return jax.shard_map(
        body, mesh=mesh, in_specs=placed, out_specs=P("row", "col"), check_vma=False
    )
```
